256 devices in a mesh: rep: 8 (over x, y_hi), fsdp: 32 (over y_lo, z, core).
Axes of the slice: x: 4, y: 4 (y_hi: 2, y_lo: 2; y = y_hi * 2 + y_lo), z: 8, core: 2. Of those that a mesh axis runs over, the one named last changes fastest.
Arguments:
- global_w: float32 [10240, 768], P('fsdp'), may hold values from -6 to 6
- momentum: float32 [10240, 768], P('fsdp'), may hold values from -3 to 3
- local_w: bfloat16 [8, 10240, 768], P('rep', 'fsdp'), may hold values from -6 to 6
- tokens: bfloat16 [8, 8192, 10240], P('rep', 'fsdp'), may hold values from -6 to 6
Outputs:
- new_global: float32 [10240, 768], P('fsdp')
- new_moment: float32 [10240, 768], P('fsdp')
- new_local: bfloat16 [8, 10240, 768], P('rep', 'fsdp')
- projected: bfloat16 [8, 8192, 768], P('rep', 'fsdp')
The draws below stay inside these ranges and needn't reach their ends.
All inputs are finite; a program needn't handle non-finite values.
Results may differ from the reference program's by a relative error of at most 0.0049.
Values may be sent and summed in bfloat16 or wider, within the bound.
No kernel may reach another device: no remote copies, remote signals or barrier semaphores. Data moves between devices by JAX's collectives and lax.ppermute only.
A program may use at most 128 MiB of HBM per device.

```python
import math
import jax
import jax.numpy as jnp
from jax import lax

D = 10240
COLS = 768
REPS = 8
TOKENS = 8192


def shard_levels(key, extent, split, smallest, high):
    def one(position, shards_of):
        heights = jax.random.uniform(jax.random.fold_in(jax.random.fold_in(key, 6), position), (shards_of,), jnp.float32, smallest / len(split), high / len(split))
        return jnp.repeat(jnp.exp(heights), extent[position] // shards_of).reshape((-1,) + (1,) * (len(extent) - position - 1))

    level = one(*split[0])
    for cut in split[1:]:
        level = level * one(*cut)
    return level


def scatter_about(key, extent, spread, limit, pieces=(), kind=jnp.bfloat16):
    drawn = spread * jax.random.normal(key, extent, jnp.float32)
    if pieces:
        drawn = drawn * shard_levels(key, extent, pieces, -0.22, 0.18)
    return jnp.clip(drawn, -limit, limit).astype(kind)


def setup_inputs(seed: int = 0) -> dict:
    streams_of = jax.random.split(jax.random.key(seed), 5)
    global_w = scatter_about(streams_of[0], (D, COLS), 1.0, 6.0, ((0, 32),), jnp.float32)
    momentum = scatter_about(streams_of[1], (D, COLS), 0.5, 3.0, ((0, 32),), jnp.float32)
    local_w = scatter_about(streams_of[2], (REPS, D, COLS), 1.0, 6.0, ((0, 8), (1, 32)))
    tokens = scatter_about(streams_of[3], (REPS, TOKENS, D), 1.0, 6.0, ((0, 8), (1, 32)))
    return {"global_w": global_w, "momentum": momentum, "local_w": local_w, "tokens": tokens}


OUTER_RATE = 0.7
MOMENT_DECAY = 0.9
KEEP_LOCAL = 0.5

def outer_update(global_part, moment_part, local_part, summed, replicas):
    gradient = summed / replicas
    new_moment = MOMENT_DECAY * moment_part + gradient
    new_global = global_part - OUTER_RATE * (gradient + MOMENT_DECAY * new_moment)
    blended = (KEEP_LOCAL * local_part.astype(jnp.float32) + (1.0 - KEEP_LOCAL) * new_global).astype(jnp.bfloat16)
    return (new_global, new_moment, blended)

def reference(global_w, momentum, local_w, tokens):

    def accumulate(running, replica_w):
        pseudo = global_w - replica_w.astype(jnp.float32)
        return (running + pseudo, None)
    summed, _ = lax.scan(accumulate, jnp.zeros(global_w.shape, jnp.float32), local_w)
    new_global, new_moment, blended = outer_update(global_w, momentum, local_w, summed, REPS)
    scaling = 1.0 / math.sqrt(D)

    def forward(operands):
        product = jnp.dot(operands[0], operands[1], preferred_element_type=jnp.float32)
        return (product * scaling).astype(jnp.bfloat16)
    projected = lax.map(forward, (tokens, blended))
    return (new_global, new_moment, blended, projected)
```

```python
import functools
import math

import jax
import jax.numpy as jnp
from jax import lax
from jax.experimental import pallas as pl
from jax.experimental.pallas import tpu as pltpu
from jax.sharding import PartitionSpec as P

D = 10240
COLS = 768
HALF = COLS // 2
REPS = 8
OUTER_RATE = 0.7
MOMENT_DECAY = 0.9
KEEP_LOCAL = 0.5

NX, NYH, NYL, NZ, NC = 4, 2, 2, 8, 2
ROWS = D // (NYL * NZ * NC)
CHIP = ROWS * NC
A = 384
B = CHIP - A
STEP = 4 * CHIP
SLICE = ROWS // NX


def rep_perm(dx, dy):
    return [
        (x * NYH + y, ((x + dx) % NX) * NYH + (y ^ dy)) for x in range(NX) for y in range(NYH)
    ]


def fsdp_perm(dy, dz, dc):
    return [
        ((y * NZ + z) * NC + c, ((y ^ dy) * NZ + (z + dz) % NZ) * NC + (c ^ dc))
        for y in range(NYL)
        for z in range(NZ)
        for c in range(NC)
    ]


def send_rep(v, dx, dy):
    return lax.ppermute(v, "rep", rep_perm(dx, dy))


def send(v, dy, dz, dc):
    return lax.ppermute(v, "fsdp", fsdp_perm(dy, dz, dc))


def pieces_of(d):
    return [(0, d), (1, d)]


ORDER = (
    pieces_of(0) + pieces_of(4)
    + pieces_of(-1) + pieces_of(1)
    + pieces_of(-2) + pieces_of(2)
    + pieces_of(-3) + pieces_of(3)
)


def reorder_kernel(tok_ref, out_ref, sems):
    me = lax.axis_index("fsdp")
    yl = me // (NZ * NC)
    z = (me // NC) % NZ
    copies = []
    for place, (flip, dz) in enumerate(ORDER):
        y = (1 - yl) if flip else yl
        shard = y * NZ + (z + dz + NZ) % NZ
        spans = ((0, 0, CHIP),) if not flip else ((A, 0, B), (0, B, A))
        for source, target, width in spans:
            copy = pltpu.make_async_copy(
                tok_ref.at[:, pl.ds(pl.multiple_of(shard * CHIP + source, 128), width)],
                out_ref.at[:, pl.ds(place * CHIP + target, width)],
                sems.at[len(copies)],
            )
            copy.start()
            copies.append(copy)
    for copy in copies:
        copy.wait()


def reorder(tokens):
    return pl.pallas_call(
        reorder_kernel,
        out_shape=jax.ShapeDtypeStruct(tokens.shape, tokens.dtype),
        in_specs=[pl.BlockSpec(memory_space=pl.ANY)],
        out_specs=pl.BlockSpec(memory_space=pl.ANY),
        scratch_shapes=[pltpu.SemaphoreType.DMA((len(ORDER) * 3 // 2,))],
        cost_estimate=pl.CostEstimate(
            flops=0, bytes_accessed=2 * tokens.size * 2, transcendentals=0
        ),
    )(tokens)


def step_kernel(spans, first, last, scale, *refs):
    arrays = len({array for array, _, _ in spans})
    toks, weights, refs = refs[:2], refs[2 : 2 + arrays], refs[2 + arrays :]
    before, outs = ((), refs) if first else (refs[:2], refs[2:])
    for which, (tok, out) in enumerate(zip(toks, outs)):
        total = None if first else before[which][...]
        at = 0
        for array, start, rows in spans:
            product = jnp.dot(
                tok[:, at : at + rows],
                weights[array][start : start + rows, :],
                preferred_element_type=jnp.float32,
            )
            total = product if total is None else total + product
            at += rows
        out[...] = (total * scale).astype(out.dtype) if last else total


def step(mine, other, weights, spans, totals, block, last):
    rows, width = mine.shape[0], sum(span[2] for span in spans)
    first = totals is None
    kind = jnp.bfloat16 if last else jnp.float32
    tok_spec = pl.BlockSpec((rows, width), lambda i: (0, block))
    whole = pl.BlockSpec(memory_space=pltpu.VMEM)
    operands = (mine, other) + tuple(weights) + (() if first else tuple(totals))
    return pl.pallas_call(
        functools.partial(step_kernel, spans, first, last, 1.0 / math.sqrt(D)),
        out_shape=[jax.ShapeDtypeStruct((rows, HALF), kind)] * 2,
        grid=(1,),
        in_specs=[tok_spec, tok_spec] + [whole] * (len(operands) - 2),
        out_specs=[whole, whole],
        compiler_params=pltpu.CompilerParams(vmem_limit_bytes=32 * 1024 * 1024),
        cost_estimate=pl.CostEstimate(
            flops=2 * 2 * rows * width * HALF,
            bytes_accessed=2 * (2 * rows * width + width * HALF) + 16 * rows * HALF,
            transcendentals=0,
        ),
    )(*operands)


def after(value, *earlier):
    return lax.optimization_barrier((value, earlier))[0]


def in_order(slices, x):
    rows = []
    for place in range(NX):
        value = slices[0]
        for k in range(1, NX):
            value = jnp.where((x - k) % NX == place, slices[k], value)
        rows.append(value)
    return jnp.concatenate(rows, axis=0)


def on_device(global_w, momentum, local_w, tokens):
    local = local_w[0]
    x = lax.axis_index("rep") // NYH
    core = lax.axis_index("fsdp") % NC

    def quarter(v, place):
        return lax.dynamic_slice(v, (place * SLICE, 0), (SLICE, COLS))

    raw = [quarter(local, x)] + [
        send_rep(quarter(local, (x + k) % NX), k, 0) for k in range(1, NX)
    ]
    global_part = quarter(global_w, x)
    four = sum(global_part - r.astype(jnp.float32) for r in raw)
    mine = reorder(after(tokens[0], four))
    other = send(mine, 0, 0, 1)
    gradient = (four + send_rep(four, 0, 1)) / REPS
    moment_part = MOMENT_DECAY * quarter(momentum, x) + gradient
    new_part = global_part - OUTER_RATE * (gradient + MOMENT_DECAY * moment_part)

    def blend(r):
        return (
            KEEP_LOCAL * r.astype(jnp.float32) + (1.0 - KEEP_LOCAL) * new_part
        ).astype(jnp.bfloat16)

    back = [blend(raw[0])] + [send_rep(blend(raw[k]), -k, 0) for k in range(1, NX)]
    back = [back[0], back[3], back[2], back[1]]
    new_local = in_order(back, x)

    left, right = new_local[:, :HALF], new_local[:, HALF:]
    keep = jnp.where(core == 0, left, right)
    got = send(jnp.where(core == 0, right, left), 0, 0, 1)
    shard = jnp.concatenate(
        [jnp.where(core == 0, keep, got), jnp.where(core == 0, got, keep)], axis=0
    )
    own_a, own_b = shard[:A], shard[A:]
    part_b = send(own_b, 1, 0, 0)
    part_a = send(after(own_a, part_b), 1, 0, 0)
    both = jnp.concatenate([own_b, part_b], axis=0)

    spans = ((0, 0, A), (1, 0, 2 * B), (2, 0, A), (3, 0, A), (4, 0, 2 * B), (2, A, A))
    totals = None
    up_a, down_a, up_b, down_b, side = own_a, own_a, both, both, part_a
    for d in range(1, 4):
        up_a, down_a = send(up_a, 0, 1, 0), send(down_a, 0, -1, 0)
        if d > 1:
            totals = step(mine, other, held, spans, totals, d - 1, False)
            up_b, down_b = after((up_b, down_b), *totals)
        up_b, down_b = send(up_b, 0, 1, 0), send(down_b, 0, -1, 0)
        side = send(after(jnp.concatenate([up_a, down_a], axis=0), side), 1, 0, 0)
        held = [up_a, up_b, side, down_a, down_b]
        if d == 2:
            gradient = after(gradient, *totals)
            sums = [gradient] + [send_rep(gradient, k, 0) for k in range(1, NX)]
    far_a = [send(up_a[: A // 2], 0, 1, 0), send(down_a[A // 2 :], 0, -1, 0)]
    far_b = [send(up_b[:B], 0, 1, 0), send(down_b[B:], 0, -1, 0)]
    far_a = jnp.concatenate(far_a, axis=0)
    far_side = send(after(far_a, side), 1, 0, 0)
    totals = step(mine, other, held, spans, totals, 3, False)

    full = in_order(sums, x)
    new_moment = MOMENT_DECAY * momentum + full
    new_global = global_w - OUTER_RATE * (full + MOMENT_DECAY * new_moment)

    weights = [own_a, both, part_a, far_a] + far_b + [far_side]
    spans = ((0, 0, A), (1, 0, 2 * B), (2, 0, A), (3, 0, A), (4, 0, B), (5, 0, B), (6, 0, A))
    own, theirs = step(mine, other, weights, spans, totals, 0, True)

    came = send(theirs, 0, 0, 1)
    projected = jnp.concatenate(
        [jnp.where(core == 0, own, came), jnp.where(core == 0, came, own)], axis=1
    )
    return (new_global, new_moment, new_local[None], projected[None])


def solution(mesh):
    return jax.shard_map(
        on_device,
        mesh=mesh,
        in_specs=(P("fsdp", None), P("fsdp", None), P("rep", "fsdp", None), P("rep", "fsdp", None)),
        out_specs=(
            P("fsdp", None),
            P("fsdp", None),
            P("rep", "fsdp", None),
            P("rep", "fsdp", None),
        ),
        check_vma=False,
    )
```

```python
import functools
import math

import jax
import jax.numpy as jnp
from jax import lax
from jax.experimental import pallas as pl
from jax.experimental.pallas import tpu as pltpu
from jax.sharding import PartitionSpec as P

D = 10240
COLS = 768
REPS = 8
OUTER_RATE = 0.7
MOMENT_DECAY = 0.9
KEEP_LOCAL = 0.5
SCALE = 1.0 / math.sqrt(D)

NX, NYH, NYL, NZ, NC = 4, 2, 2, 8, 2
ROWS = D // (NYL * NZ * NC)
CHIP = ROWS * NC
SLICE = ROWS // NX
FAR = ROWS // 2
BIG = 60 * 1024 * 1024
LONG = 30_000_000_000
CHUNKS = 3
WIDTH = COLS // CHUNKS


def rep_perm(dx, dy):
    return [
        (x * NYH + y, ((x + dx) % NX) * NYH + (y ^ dy)) for x in range(NX) for y in range(NYH)
    ]


def send_rep(v, dx, dy, name):
    with jax.named_scope(name):
        return lax.ppermute(v, "rep", rep_perm(dx, dy))


def send(v, to, name, cores=(0, 1)):
    perm = []
    for y in range(NYL):
        for z in range(NZ):
            for c in cores:
                ty, tz, tc = to(y, z, c)
                perm.append(((y * NZ + z) * NC + c, (ty * NZ + tz % NZ) * NC + tc))
    with jax.named_scope(name):
        return lax.ppermute(v, "fsdp", perm)


def to_core(y, z, c):
    return y, z, 1 - c


def to_side(y, z, c):
    return 1 - y, z, c


def to_cross(y, z, c):
    return 1 - y, z, 1 - c


def to_ring(y, z, c):
    return y, (z - 1 if c else z + 1), c


def fence_kernel(*refs):
    del refs


def fence(values, *earlier):
    anywhere = pl.BlockSpec(memory_space=pl.ANY)
    operands = tuple(values) + earlier
    return pl.pallas_call(
        fence_kernel,
        out_shape=[jax.ShapeDtypeStruct(v.shape, v.dtype) for v in values],
        in_specs=[anywhere] * len(operands),
        out_specs=[anywhere] * len(values),
        input_output_aliases={i: i for i in range(len(values))},
        compiler_params=pltpu.CompilerParams(vmem_limit_bytes=1024 * 1024),
        cost_estimate=pl.CostEstimate(flops=LONG, bytes_accessed=4096, transcendentals=0),
    )(*operands)


def in_order(slices, x):
    rows = []
    for place in range(NX):
        value = slices[0]
        for k in range(1, NX):
            value = jnp.where((x - k) % NX == place, slices[k], value)
        rows.append(value)
    return jnp.concatenate(rows, axis=0)


def dot(a, b):
    return jnp.dot(a, b, preferred_element_type=jnp.float32)


def either(core, first, second):
    return jnp.where(core == 0, first, second)


def stack(*rows):
    return jnp.concatenate(rows, axis=0)


HERE = pl.BlockSpec(memory_space=pl.ANY)
WHOLE = pl.BlockSpec(memory_space=pltpu.VMEM)
SCALARS = pl.BlockSpec(memory_space=pltpu.SMEM)

A_ROWS, B_ROWS = (0, ROWS), (ROWS, 0)
A_NEAR, A_REST = (0, ROWS + FAR), (FAR, ROWS)
B_NEAR, B_REST = (ROWS, FAR), (ROWS + FAR, 0)


def product_kernel(slots, parts, near, empty, totals, counts, where_ref, *refs):
    core = where_ref[0]
    split = [0]
    for count in counts:
        split.append(split[-1] + count)
    tokens, arrays, before, outs = (refs[i:j] for i, j in zip(split, split[1:]))
    tok, weight, total, sems = refs[split[-1] :]
    rows = tokens[0].shape[0]
    started = []

    def start(source, target):
        copy = pltpu.make_async_copy(source, target, sems.at[len(started)])
        copy.start()
        started.append(copy)

    def spot(slot, place, size):
        at = slot * CHIP + either(core, place[0], place[1])
        return pl.ds(pl.multiple_of(at, 16), size)

    def extra(own, n):
        last, cols = (len(slots) - 1) * CHIP, pl.ds(n * WIDTH, WIDTH)
        pair = (arrays[-4], arrays[-3]) if own else (arrays[-2], arrays[-1])
        return [
            pltpu.make_async_copy(
                array.at[:, cols],
                weight.at[n, pl.ds(last + i * ROWS, ROWS)],
                sems.at[sems.shape[0] - 1 - 2 * n - i],
            )
            for i, array in enumerate(pair)
        ]

    for s, slot in enumerate(slots):
        span = pl.ds(pl.multiple_of(where_ref[slot] * CHIP, 128), CHIP)
        for i, ref in enumerate(tokens):
            start(ref.at[:, span], tok.at[pl.ds(i * rows, rows), pl.ds(s * CHIP, CHIP)])
    ends = []
    for n in range(CHUNKS):
        cols = pl.ds(n * WIDTH, WIDTH)
        for array, first, size, slot, place in parts:
            start(
                arrays[array].at[pl.ds(first, size), cols],
                weight.at[n, spot(slot, place, size)],
            )
        for i, ref in enumerate(before):
            start(ref.at[:, cols], total.at[n, pl.ds(i * rows, rows)])
        if near:

            @pl.when(core == 0)
            def _(n=n):
                for copy in extra(True, n):
                    copy.start()

            @pl.when(core == 1)
            def _(n=n):
                for copy in extra(False, n):
                    copy.start()

        ends.append(len(started))
    for n in range(CHUNKS):
        for slot, place in empty:
            weight[n, spot(slot, place, FAR), :] = jnp.zeros((FAR, WIDTH), jnp.bfloat16)
    done = 0
    for n in range(CHUNKS):
        for copy in started[done : ends[n]]:
            copy.wait()
        done = ends[n]
        if near:
            for copy in extra(True, n):
                copy.wait()
        value = jnp.dot(tok[...], weight[n], preferred_element_type=jnp.float32)
        if totals:
            value = value + total[n]
        for i, out in enumerate(outs):
            out[:, n * WIDTH : (n + 1) * WIDTH] = value[i * rows : (i + 1) * rows].astype(out.dtype)


def product_step(where, slots, tokens, arrays, parts, near, empty, totals, final=False):
    rows, outs, depth = tokens[0].shape[0], len(tokens), len(slots) * CHIP
    kinds = (jnp.float32, jnp.bfloat16 if final else jnp.float32)
    operands = tuple(tokens) + tuple(arrays) + tuple(near) + tuple(totals)
    counts = (outs, len(arrays) + len(near), len(totals), outs)
    copies = len(slots) * outs + CHUNKS * (len(parts) + len(totals) + 2)
    return pl.pallas_call(
        functools.partial(product_kernel, slots, parts, bool(near), empty, bool(totals), counts),
        out_shape=[jax.ShapeDtypeStruct((rows, COLS), k) for k in kinds],
        in_specs=[SCALARS] + [HERE] * len(operands),
        out_specs=[WHOLE] * outs,
        scratch_shapes=[
            pltpu.VMEM((outs * rows, depth), jnp.bfloat16),
            pltpu.VMEM((CHUNKS, depth, WIDTH), jnp.bfloat16),
            pltpu.VMEM((CHUNKS, outs * rows, WIDTH), jnp.float32),
            pltpu.SemaphoreType.DMA((copies,)),
        ],
        compiler_params=pltpu.CompilerParams(vmem_limit_bytes=BIG),
        cost_estimate=pl.CostEstimate(
            flops=LONG,
            bytes_accessed=depth * (2 * outs * rows + 2 * COLS) + 8 * rows * COLS,
            transcendentals=0,
        ),
    )(where, *operands)


def on_device(global_w, momentum, local_w, tokens):
    local = local_w[0]
    x = lax.axis_index("rep") // NYH
    me = lax.axis_index("fsdp")
    core, z, y = me % NC, (me // NC) % NZ, me // (NC * NZ)

    def own_at(d):
        return y * NZ + either(core, z - d, z + d) % NZ

    def part_at(d):
        return (1 - y) * NZ + either(core, z - d, z + d) % NZ

    near_at = either(core, y, 1 - y) * NZ + z

    where = [core, near_at] + [at(d) for d in range(1, 5) for at in (own_at, part_at)]
    where = jnp.stack(where).astype(jnp.int32)

    def quarter(v, place):
        return lax.dynamic_slice(v, (place * SLICE, 0), (SLICE, COLS))

    raw = [quarter(local, x)] + [
        send_rep(quarter(local, (x + k) % NX), k, 0, "quarters") for k in range(1, NX)
    ]
    global_part, moment_part = quarter(global_w, x), quarter(momentum, x)
    four = sum(global_part - r.astype(jnp.float32) for r in raw)
    gradient = (four + send_rep(four, 0, 1, "four")) / REPS
    mine = tokens[0]
    other = send(mine, to_core, "other")

    def update(global_rows, moment_rows, gradient):
        new_moment = MOMENT_DECAY * moment_rows + gradient
        return global_rows - OUTER_RATE * (gradient + MOMENT_DECAY * new_moment), new_moment

    def blend(local_rows, new_rows):
        return (
            KEEP_LOCAL * local_rows.astype(jnp.float32) + (1.0 - KEEP_LOCAL) * new_rows
        ).astype(jnp.bfloat16)

    new_part, _ = update(global_part, moment_part, gradient)
    home = [blend(r, new_part) for r in raw]
    back = [home[0]] + [send_rep(home[NX - k], k, 0, "home") for k in range(1, NX)]
    shard = in_order(back, x)

    def near_half(v):
        return either(core, v[:FAR], v[FAR:])

    tokens = (mine, other)
    a = shard
    b = send(shard, to_core, "b")
    a1 = send(a, to_ring, "a1")
    part_b = send(shard, to_cross, "part_b")
    (b,) = fence((b,))
    b1 = send(b, to_ring, "b1")
    (a1,) = fence((a1,), b)
    a2 = send(a1, to_ring, "a2")
    side1 = send(a1, to_side, "side1")
    (part_b,) = fence((part_b,), a1)
    part_b1 = send(part_b, to_ring, "part_b1")
    side = send(shard, to_side, "side", (1,))
    (b1,) = fence((b1,), part_b)
    b2 = send(b1, to_ring, "b2")
    (a2,) = fence((a2,), b1)
    a3 = send(a2, to_ring, "a3")
    side2 = send(a2, to_side, "side2")
    (part_b1,) = fence((part_b1,), a2)
    part_b2 = send(part_b1, to_ring, "part_b2")
    totals = product_step(
        where, (2, 1), tokens, (a1, b1),
        ((0, 0, ROWS, 0, A_ROWS), (1, 0, ROWS, 0, B_ROWS)),
        (a, b, part_b, side), (), (),
    )
    b2, *totals = fence((b2, *totals), part_b1)
    b3 = send(b2, to_ring, "b3")
    (a3,) = fence((a3,), b2)
    a4 = send(near_half(a3), to_ring, "a4")
    side3 = send(a3, to_side, "side3")
    (gradient,) = fence((gradient,), a3)
    sums = [send_rep(gradient, k, 0, "gradient") for k in range(1, NX)]
    (part_b2,) = fence((part_b2,), a3)
    part_b3 = send(part_b2, to_ring, "part_b3")
    totals = product_step(
        where, (4, 5, 3), tokens,
        (a2, b2, side2, part_b2, side1, part_b1),
        (
            (0, 0, ROWS, 0, A_ROWS), (1, 0, ROWS, 0, B_ROWS),
            (2, 0, ROWS, 1, A_ROWS), (3, 0, ROWS, 1, B_ROWS),
            (4, 0, ROWS, 2, A_ROWS), (5, 0, ROWS, 2, B_ROWS),
        ),
        (), (), totals,
    )
    b3, *totals = fence((b3, *totals), part_b2)
    b4 = send(near_half(b3), to_ring, "b4")
    (a4,) = fence((a4,), b3)
    far_side = send(a4, to_side, "far_side")
    sums = [gradient] + list(fence(sums, a4))

    full = in_order(sums, x)
    new_global, new_moment = update(global_w, momentum, full)
    new_local = blend(local, new_global)

    (part_b3,) = fence((part_b3,), new_local)
    part_b4 = send(near_half(part_b3), to_ring, "part_b4")
    totals = product_step(
        where, (6, 7), tokens, (a3, b3, side3, part_b3),
        (
            (0, 0, ROWS, 0, A_ROWS), (1, 0, ROWS, 0, B_ROWS),
            (2, 0, ROWS, 1, A_ROWS), (3, 0, ROWS, 1, B_ROWS),
        ),
        (), (), totals,
    )
    total, late = product_step(
        where, (8, 9), tokens, (a4, b4, far_side, part_b4),
        (
            (0, 0, FAR, 0, A_NEAR), (1, 0, FAR, 0, B_NEAR),
            (2, 0, FAR, 1, A_NEAR), (3, 0, FAR, 1, B_NEAR),
        ),
        (), ((0, A_REST), (0, B_REST), (1, A_REST), (1, B_REST)), totals, True,
    )
    late = send(late, to_core, "late")
    projected = ((total + late.astype(jnp.float32)) * SCALE).astype(jnp.bfloat16)
    return (new_global, new_moment, new_local[None], projected[None])


def solution(mesh):
    return jax.shard_map(
        on_device,
        mesh=mesh,
        in_specs=(P("fsdp", None), P("fsdp", None), P("rep", "fsdp", None), P("rep", "fsdp", None)),
        out_specs=(
            P("fsdp", None),
            P("fsdp", None),
            P("rep", "fsdp", None),
            P("rep", "fsdp", None),
        ),
        check_vma=False,
    )
```

```python
import functools
import math

import jax
import jax.numpy as jnp
from jax import lax
from jax.experimental import pallas as pl
from jax.experimental.pallas import tpu as pltpu
from jax.sharding import PartitionSpec as P

D = 10240
COLS = 768
REPS = 8
OUTER_RATE = 0.7
MOMENT_DECAY = 0.9
KEEP_LOCAL = 0.5
SCALE = 1.0 / math.sqrt(D)

NX, NYH, NYL, NZ, NC = 4, 2, 2, 8, 2
ROWS = D // (NYL * NZ * NC)
CHIP = ROWS * NC
SLICE = ROWS // NX
FAR = ROWS // 2
BIG = 24 * 1024 * 1024
LONG = 30_000_000_000
CHUNKS = 1
WIDTH = COLS // CHUNKS


def rep_perm(dx, dy):
    return [
        (x * NYH + y, ((x + dx) % NX) * NYH + (y ^ dy)) for x in range(NX) for y in range(NYH)
    ]


def send_rep(v, dx, dy, name):
    with jax.named_scope(name):
        return lax.ppermute(v, "rep", rep_perm(dx, dy))


def send(v, to, name, cores=(0, 1)):
    perm = []
    for y in range(NYL):
        for z in range(NZ):
            for c in cores:
                ty, tz, tc = to(y, z, c)
                perm.append(((y * NZ + z) * NC + c, (ty * NZ + tz % NZ) * NC + tc))
    with jax.named_scope(name):
        return lax.ppermute(v, "fsdp", perm)


def to_core(y, z, c):
    return y, z, 1 - c


def to_side(y, z, c):
    return 1 - y, z, c


def to_cross(y, z, c):
    return 1 - y, z, 1 - c


def to_ring(y, z, c):
    return y, (z - 1 if c else z + 1), c


def fence_kernel(*refs):
    del refs


def fence(values, *earlier):
    anywhere = pl.BlockSpec(memory_space=pl.ANY)
    operands = tuple(values) + earlier
    return pl.pallas_call(
        fence_kernel,
        out_shape=[jax.ShapeDtypeStruct(v.shape, v.dtype) for v in values],
        in_specs=[anywhere] * len(operands),
        out_specs=[anywhere] * len(values),
        input_output_aliases={i: i for i in range(len(values))},
        compiler_params=pltpu.CompilerParams(vmem_limit_bytes=1024 * 1024),
        cost_estimate=pl.CostEstimate(flops=LONG, bytes_accessed=4096, transcendentals=0),
    )(*operands)


def in_order_kernel(*refs):
    slices, out, sems = refs[:NX], refs[NX], refs[NX + 1]
    x = lax.axis_index("rep") // NYH
    started = []
    for k, ref in enumerate(slices):
        at = ((x + NX - k) % NX) * SLICE
        copy = pltpu.make_async_copy(
            ref, out.at[pl.ds(pl.multiple_of(at, 16), SLICE)], sems.at[k]
        )
        copy.start()
        started.append(copy)
    for copy in started:
        copy.wait()


def in_order(slices):
    anywhere = pl.BlockSpec(memory_space=pl.ANY)
    return pl.pallas_call(
        in_order_kernel,
        out_shape=jax.ShapeDtypeStruct((ROWS, COLS), slices[0].dtype),
        in_specs=[anywhere] * NX,
        out_specs=anywhere,
        scratch_shapes=[pltpu.SemaphoreType.DMA((NX,))],
        compiler_params=pltpu.CompilerParams(vmem_limit_bytes=1024 * 1024),
        cost_estimate=pl.CostEstimate(
            flops=0, bytes_accessed=4 * ROWS * COLS, transcendentals=0
        ),
    )(*slices)


def either(core, first, second):
    return jnp.where(core == 0, first, second)


def stack(*rows):
    return jnp.concatenate(rows, axis=0)


HERE = pl.BlockSpec(memory_space=pl.ANY)
WHOLE = pl.BlockSpec(memory_space=pltpu.VMEM)

A_ROWS, B_ROWS = (0, ROWS), (ROWS, 0)
A_NEAR, A_REST = (0, ROWS + FAR), (FAR, ROWS)
B_NEAR, B_REST = (ROWS, FAR), (ROWS + FAR, 0)


def product_kernel(slots, parts, empty, totals, counts, *refs):
    me = lax.axis_index("fsdp")
    core, z, y = me % NC, (me // NC) % NZ, me // (NC * NZ)
    split = [0]
    for count in counts:
        split.append(split[-1] + count)
    tokens, arrays, before, _, outs = (refs[i:j] for i, j in zip(split, split[1:]))
    mark, tok, weight, total, sems = refs[split[-1] :]
    mark[...] = jnp.zeros(mark.shape, mark.dtype)
    rows = tokens[0].shape[0]
    started = []

    def start(source, target):
        copy = pltpu.make_async_copy(source, target, sems.at[len(started)])
        copy.start()
        started.append(copy)

    def spot(slot, place, size):
        at = slot * CHIP + either(core, place[0], place[1])
        return pl.ds(pl.multiple_of(at, 16), size)

    for s, slot in enumerate(slots):
        flip, d = slot
        shard = (1 - y if flip else y) * NZ + (z + either(core, NZ - d, d)) % NZ
        span = pl.ds(pl.multiple_of(shard * CHIP, 128), CHIP)
        for i, ref in enumerate(tokens):
            start(ref.at[:, span], tok.at[pl.ds(i * rows, rows), pl.ds(s * CHIP, CHIP)])
    ends = []
    for n in range(CHUNKS):
        cols = pl.ds(n * WIDTH, WIDTH)
        for array, first, size, slot, place in parts:
            start(
                arrays[array].at[pl.ds(first, size), cols],
                weight.at[n, spot(slot, place, size)],
            )
        for i, ref in enumerate(before):
            start(ref.at[:, cols], total.at[n, pl.ds(i * rows, rows)])
        ends.append(len(started))
    for n in range(CHUNKS):
        for slot, place, size in empty:
            weight[n, spot(slot, place, size), :] = jnp.zeros((size, WIDTH), jnp.bfloat16)
    done = 0
    for n in range(CHUNKS):
        for copy in started[done : ends[n]]:
            copy.wait()
        done = ends[n]
        value = jnp.dot(tok[...], weight[n], preferred_element_type=jnp.float32)
        if totals:
            value = value + total[n]
        for i, out in enumerate(outs):
            out[:, n * WIDTH : (n + 1) * WIDTH] = value[i * rows : (i + 1) * rows].astype(out.dtype)


def product_step(slots, tokens, arrays, parts, empty, totals, earlier=(), final=False):
    rows, outs, depth = tokens[0].shape[0], len(tokens), len(slots) * CHIP
    kinds = (jnp.float32, jnp.bfloat16 if final else jnp.float32)
    operands = tuple(tokens) + tuple(arrays) + tuple(totals) + tuple(earlier)
    counts = (outs, len(arrays), len(totals), len(earlier), outs)
    copies = len(slots) * outs + CHUNKS * (len(parts) + len(totals))
    return pl.pallas_call(
        functools.partial(product_kernel, slots, parts, empty, bool(totals), counts),
        out_shape=[jax.ShapeDtypeStruct((rows, COLS), k) for k in kinds]
        + [jax.ShapeDtypeStruct((8, 128), jnp.float32)],
        in_specs=[HERE] * len(operands),
        out_specs=[WHOLE] * (outs + 1),
        scratch_shapes=[
            pltpu.VMEM((outs * rows, depth), jnp.bfloat16),
            pltpu.VMEM((CHUNKS, depth, WIDTH), jnp.bfloat16),
            pltpu.VMEM((CHUNKS, outs * rows, WIDTH), jnp.float32),
            pltpu.SemaphoreType.DMA((copies,)),
        ],
        compiler_params=pltpu.CompilerParams(vmem_limit_bytes=BIG),
        cost_estimate=pl.CostEstimate(
            flops=LONG,
            bytes_accessed=depth * (2 * outs * rows + 2 * COLS) + 8 * rows * COLS,
            transcendentals=0,
        ),
    )(*operands)


def update(global_rows, moment_rows, gradient):
    new_moment = MOMENT_DECAY * moment_rows + gradient
    return global_rows - OUTER_RATE * (gradient + MOMENT_DECAY * new_moment), new_moment


def blend(local_rows, new_rows):
    return (
        KEEP_LOCAL * local_rows.astype(jnp.float32) + (1.0 - KEEP_LOCAL) * new_rows
    ).astype(jnp.bfloat16)


def blend_kernel(one, two, global_ref, moment_ref, *refs):
    raw, homes, gradient_ref = refs[:NX], refs[NX : 2 * NX], refs[2 * NX]
    gradient = (one[...] + two[...]) / REPS
    gradient_ref[...] = gradient
    new_part, _ = update(global_ref[...], moment_ref[...], gradient)
    for local_ref, home in zip(raw, homes):
        home[...] = blend(local_ref[...], new_part)


def local_call(kernel, kinds, *operands):
    whole = pl.BlockSpec(memory_space=pltpu.VMEM)
    return pl.pallas_call(
        kernel,
        out_shape=[jax.ShapeDtypeStruct((SLICE, COLS), kind) for kind in kinds],
        in_specs=[whole] * len(operands),
        out_specs=[whole] * len(kinds),
        compiler_params=pltpu.CompilerParams(vmem_limit_bytes=8 * 1024 * 1024),
    )(*operands)


def on_device(global_w, momentum, local_w, tokens):
    local = local_w[0]
    core = lax.axis_index("fsdp") % NC

    x = lax.axis_index("rep") // NYH

    def quarter(v, place):
        return lax.dynamic_slice(v, (place * SLICE, 0), (SLICE, COLS))

    raw = [quarter(local, x)] + [
        send_rep(quarter(local, (x + k) % NX), k, 0, "quarters") for k in range(1, NX)
    ]
    global_part, moment_part = quarter(global_w, x), quarter(momentum, x)
    four = sum(global_part - r.astype(jnp.float32) for r in raw)
    four, global_part, moment_part, raw[0] = lax.optimization_barrier(
        (four, global_part, moment_part, raw[0])
    )
    other_four = send_rep(four, 0, 1, "four")
    mine = tokens[0]
    other = send(mine, to_core, "other")
    *home, gradient = local_call(
        blend_kernel, [jnp.bfloat16] * NX + [jnp.float32],
        four, other_four, global_part, moment_part, *raw,
    )
    back = [home[0]] + [send_rep(home[NX - k], k, 0, "home") for k in range(1, NX)]
    shard = in_order(back)

    def near_half(v):
        return either(core, v[:FAR], v[FAR:])

    tokens = (mine, other)
    a = shard
    b = send(shard, to_core, "b")
    a1 = send(a, to_ring, "a1")
    part_b = send(shard, to_cross, "part_b")
    (b,) = fence((b,))
    b1 = send(b, to_ring, "b1")
    (a1,) = fence((a1,), b)
    a2 = send(a1, to_ring, "a2")
    side1 = send(a1, to_side, "side1")
    (part_b,) = fence((part_b,), a1)
    part_b1 = send(part_b, to_ring, "part_b1")
    (b1,) = fence((b1,), part_b)
    b2 = send(b1, to_ring, "b2")
    (a2,) = fence((a2,), b1)
    a3 = send(a2, to_ring, "a3")
    side2 = send(a2, to_side, "side2")
    (part_b1,) = fence((part_b1,), a2)
    part_b2 = send(part_b1, to_ring, "part_b2")
    *totals, mark = product_step(
        ((0, 1), (0, 0), (1, 0)), tokens, (a1, b1, a, part_b),
        ((0, 0, ROWS, 0, A_ROWS), (1, 0, ROWS, 0, B_ROWS), (2, 0, ROWS, 1, A_ROWS), (3, 0, ROWS, 2, B_ROWS)),
        ((1, B_ROWS, ROWS), (2, A_ROWS, ROWS)), (),
    )
    (b2,) = fence((b2,), part_b1, mark)
    b3 = send(b2, to_ring, "b3")
    (a3,) = fence((a3,), b2)
    a4 = send(near_half(a3), to_ring, "a4")
    side3 = send(a3, to_side, "side3")
    (gradient,) = fence((gradient,), a3)
    sums = [send_rep(gradient, k, 0, "gradient") for k in range(1, NX)]
    (part_b2,) = fence((part_b2,), a3)
    part_b3 = send(part_b2, to_ring, "part_b3")
    *totals, mark = product_step(
        ((0, 2), (1, 2), (1, 1)), tokens,
        (a2, b2, side2, part_b2, side1, part_b1),
        (
            (0, 0, ROWS, 0, A_ROWS), (1, 0, ROWS, 0, B_ROWS),
            (2, 0, ROWS, 1, A_ROWS), (3, 0, ROWS, 1, B_ROWS),
            (4, 0, ROWS, 2, A_ROWS), (5, 0, ROWS, 2, B_ROWS),
        ),
        (), totals,
    )
    (b3,) = fence((b3,), part_b2, a4, mark)
    b4 = send(near_half(b3), to_ring, "b4")
    far_side = send(a4, to_side, "far_side")
    (part_b3,) = fence((part_b3,), b3, side3)
    part_b4 = send(near_half(part_b3), to_ring, "part_b4")
    *totals, mark = product_step(
        ((0, 3), (1, 3)), tokens, (a3, b3, side3, part_b3),
        (
            (0, 0, ROWS, 0, A_ROWS), (1, 0, ROWS, 0, B_ROWS),
            (2, 0, ROWS, 1, A_ROWS), (3, 0, ROWS, 1, B_ROWS),
        ),
        (), totals,
    )
    total, late, _ = product_step(
        ((0, 4), (1, 4)), tokens, (a4, b4, far_side, part_b4),
        (
            (0, 0, FAR, 0, A_NEAR), (1, 0, FAR, 0, B_NEAR),
            (2, 0, FAR, 1, A_NEAR), (3, 0, FAR, 1, B_NEAR),
        ),
        tuple((s, place, FAR) for s in range(2) for place in (A_REST, B_REST)), totals, final=True,
    )
    late = send(late, to_core, "late")

    new_global, new_moment = update(global_w, momentum, in_order([gradient, *sums]))
    new_local = blend(local, new_global)
    projected = ((total + late.astype(jnp.float32)) * SCALE).astype(jnp.bfloat16)
    return (new_global, new_moment, new_local[None], projected[None])


def solution(mesh):
    return jax.shard_map(
        on_device,
        mesh=mesh,
        in_specs=(P("fsdp", None), P("fsdp", None), P("rep", "fsdp", None), P("rep", "fsdp", None)),
        out_specs=(
            P("fsdp", None),
            P("fsdp", None),
            P("rep", "fsdp", None),
            P("rep", "fsdp", None),
        ),
        check_vma=False,
    )
```

```python
import functools
import math

import jax
import jax.numpy as jnp
from jax import lax
from jax.experimental import pallas as pl
from jax.experimental.pallas import tpu as pltpu
from jax.sharding import PartitionSpec as P

D = 10240
COLS = 768
REPS = 8
OUTER_RATE = 0.7
MOMENT_DECAY = 0.9
KEEP_LOCAL = 0.5
SCALE = 1.0 / math.sqrt(D)

NX, NYH, NYL, NZ, NC = 4, 2, 2, 8, 2
ROWS = D // (NYL * NZ * NC)
CHIP = ROWS * NC
SLICE = ROWS // NX
FAR = ROWS // 2
BIG = 24 * 1024 * 1024
LONG = 30_000_000_000
CHUNKS = 1
WIDTH = COLS // CHUNKS


def rep_perm(dx, dy):
    return [
        (x * NYH + y, ((x + dx) % NX) * NYH + (y ^ dy)) for x in range(NX) for y in range(NYH)
    ]


def send_rep(v, dx, dy, name):
    with jax.named_scope(name):
        return lax.ppermute(v, "rep", rep_perm(dx, dy))


def send(v, to, name, cores=(0, 1)):
    perm = []
    for y in range(NYL):
        for z in range(NZ):
            for c in cores:
                ty, tz, tc = to(y, z, c)
                perm.append(((y * NZ + z) * NC + c, (ty * NZ + tz % NZ) * NC + tc))
    with jax.named_scope(name):
        return lax.ppermute(v, "fsdp", perm)


def to_core(y, z, c):
    return y, z, 1 - c


def to_side(y, z, c):
    return 1 - y, z, c


def to_cross(y, z, c):
    return 1 - y, z, 1 - c


def to_ring(y, z, c):
    return y, (z - 1 if c else z + 1), c


def fence_kernel(*refs):
    del refs


def fence(values, *earlier):
    anywhere = pl.BlockSpec(memory_space=pl.ANY)
    operands = tuple(values) + earlier
    return pl.pallas_call(
        fence_kernel,
        out_shape=[jax.ShapeDtypeStruct(v.shape, v.dtype) for v in values],
        in_specs=[anywhere] * len(operands),
        out_specs=[anywhere] * len(values),
        input_output_aliases={i: i for i in range(len(values))},
        compiler_params=pltpu.CompilerParams(vmem_limit_bytes=1024 * 1024),
        cost_estimate=pl.CostEstimate(flops=LONG, bytes_accessed=4096, transcendentals=0),
    )(*operands)


def in_order_kernel(*refs):
    slices, out, sems = refs[:NX], refs[NX], refs[NX + 1]
    x = lax.axis_index("rep") // NYH
    started = []
    for k, ref in enumerate(slices):
        at = ((x + NX - k) % NX) * SLICE
        copy = pltpu.make_async_copy(
            ref, out.at[pl.ds(pl.multiple_of(at, 16), SLICE)], sems.at[k]
        )
        copy.start()
        started.append(copy)
    for copy in started:
        copy.wait()


def in_order(slices):
    anywhere = pl.BlockSpec(memory_space=pl.ANY)
    return pl.pallas_call(
        in_order_kernel,
        out_shape=jax.ShapeDtypeStruct((ROWS, COLS), slices[0].dtype),
        in_specs=[anywhere] * NX,
        out_specs=anywhere,
        scratch_shapes=[pltpu.SemaphoreType.DMA((NX,))],
        compiler_params=pltpu.CompilerParams(vmem_limit_bytes=1024 * 1024),
        cost_estimate=pl.CostEstimate(
            flops=0, bytes_accessed=4 * ROWS * COLS, transcendentals=0
        ),
    )(*slices)


def either(core, first, second):
    return jnp.where(core == 0, first, second)


def stack(*rows):
    return jnp.concatenate(rows, axis=0)


HERE = pl.BlockSpec(memory_space=pl.ANY)
WHOLE = pl.BlockSpec(memory_space=pltpu.VMEM)

A_ROWS, B_ROWS = (0, ROWS), (ROWS, 0)
A_NEAR, A_REST = (0, ROWS + FAR), (FAR, ROWS)
B_NEAR, B_REST = (ROWS, FAR), (ROWS + FAR, 0)


def product_kernel(slots, parts, empty, totals, counts, *refs):
    me = lax.axis_index("fsdp")
    core, z, y = me % NC, (me // NC) % NZ, me // (NC * NZ)
    split = [0]
    for count in counts:
        split.append(split[-1] + count)
    tokens, arrays, before, _, outs = (refs[i:j] for i, j in zip(split, split[1:]))
    mark, tok, weight, total, sems = refs[split[-1] :]
    mark[...] = jnp.zeros(mark.shape, mark.dtype)
    rows = tokens[0].shape[0]
    started = []

    def start(source, target):
        copy = pltpu.make_async_copy(source, target, sems.at[len(started)])
        copy.start()
        started.append(copy)

    def spot(slot, place, size):
        at = slot * CHIP + either(core, place[0], place[1])
        return pl.ds(pl.multiple_of(at, 16), size)

    for s, slot in enumerate(slots):
        flip, d = slot
        shard = (1 - y if flip else y) * NZ + (z + either(core, NZ - d, d)) % NZ
        span = pl.ds(pl.multiple_of(shard * CHIP, 128), CHIP)
        for i, ref in enumerate(tokens):
            start(ref.at[:, span], tok.at[pl.ds(i * rows, rows), pl.ds(s * CHIP, CHIP)])
    ends = []
    for n in range(CHUNKS):
        cols = pl.ds(n * WIDTH, WIDTH)
        for array, first, size, slot, place in parts:
            start(
                arrays[array].at[pl.ds(first, size), cols],
                weight.at[n, spot(slot, place, size)],
            )
        for i, ref in enumerate(before):
            start(ref.at[:, cols], total.at[n, pl.ds(i * rows, rows)])
        ends.append(len(started))
    for n in range(CHUNKS):
        for slot, place, size in empty:
            weight[n, spot(slot, place, size), :] = jnp.zeros((size, WIDTH), jnp.bfloat16)
    done = 0
    for n in range(CHUNKS):
        for copy in started[done : ends[n]]:
            copy.wait()
        done = ends[n]
        value = jnp.dot(tok[...], weight[n], preferred_element_type=jnp.float32)
        if totals:
            value = value + total[n]
        for i, out in enumerate(outs):
            out[:, n * WIDTH : (n + 1) * WIDTH] = value[i * rows : (i + 1) * rows].astype(out.dtype)


def product_step(slots, tokens, arrays, parts, empty, totals, earlier=(), final=False):
    rows, outs, depth = tokens[0].shape[0], len(tokens), len(slots) * CHIP
    kinds = (jnp.float32, jnp.bfloat16 if final else jnp.float32)
    operands = tuple(tokens) + tuple(arrays) + tuple(totals) + tuple(earlier)
    counts = (outs, len(arrays), len(totals), len(earlier), outs)
    copies = len(slots) * outs + CHUNKS * (len(parts) + len(totals))
    return pl.pallas_call(
        functools.partial(product_kernel, slots, parts, empty, bool(totals), counts),
        out_shape=[jax.ShapeDtypeStruct((rows, COLS), k) for k in kinds]
        + [jax.ShapeDtypeStruct((8, 128), jnp.float32)],
        in_specs=[HERE] * len(operands),
        out_specs=[WHOLE] * (outs + 1),
        scratch_shapes=[
            pltpu.VMEM((outs * rows, depth), jnp.bfloat16),
            pltpu.VMEM((CHUNKS, depth, WIDTH), jnp.bfloat16),
            pltpu.VMEM((CHUNKS, outs * rows, WIDTH), jnp.float32),
            pltpu.SemaphoreType.DMA((copies,)),
        ],
        compiler_params=pltpu.CompilerParams(vmem_limit_bytes=BIG),
        cost_estimate=pl.CostEstimate(
            flops=LONG,
            bytes_accessed=depth * (2 * outs * rows + 2 * COLS) + 8 * rows * COLS,
            transcendentals=0,
        ),
    )(*operands)


def update(global_rows, moment_rows, gradient):
    new_moment = MOMENT_DECAY * moment_rows + gradient
    return global_rows - OUTER_RATE * (gradient + MOMENT_DECAY * new_moment), new_moment


def blend(local_rows, new_rows):
    return (
        KEEP_LOCAL * local_rows.astype(jnp.float32) + (1.0 - KEEP_LOCAL) * new_rows
    ).astype(jnp.bfloat16)


def blend_kernel(one, two, global_ref, moment_ref, *refs):
    raw, homes, gradient_ref = refs[:NX], refs[NX : 2 * NX], refs[2 * NX]
    gradient = (one[...] + two[...]) / REPS
    gradient_ref[...] = gradient
    new_part, _ = update(global_ref[...], moment_ref[...], gradient)
    for local_ref, home in zip(raw, homes):
        home[...] = blend(local_ref[...], new_part)


def local_call(kernel, kinds, *operands):
    whole = pl.BlockSpec(memory_space=pltpu.VMEM)
    return pl.pallas_call(
        kernel,
        out_shape=[jax.ShapeDtypeStruct((SLICE, COLS), kind) for kind in kinds],
        in_specs=[whole] * len(operands),
        out_specs=[whole] * len(kinds),
        compiler_params=pltpu.CompilerParams(vmem_limit_bytes=8 * 1024 * 1024),
    )(*operands)


def on_device(global_w, momentum, local_w, tokens):
    local = local_w[0]
    core = lax.axis_index("fsdp") % NC

    x = lax.axis_index("rep") // NYH

    def quarter(v, place):
        return lax.dynamic_slice(v, (place * SLICE, 0), (SLICE, COLS))

    raw = [quarter(local, x)] + [
        send_rep(quarter(local, (x + k) % NX), k, 0, "quarters") for k in range(1, NX)
    ]
    global_part, moment_part = quarter(global_w, x), quarter(momentum, x)
    four = sum(global_part - r.astype(jnp.float32) for r in raw)
    four, global_part, moment_part, raw[0] = lax.optimization_barrier(
        (four, global_part, moment_part, raw[0])
    )
    other_four = send_rep(four, 0, 1, "four")
    mine = tokens[0]
    other = send(mine, to_core, "other")
    *home, gradient = local_call(
        blend_kernel, [jnp.bfloat16] * NX + [jnp.float32],
        four, other_four, global_part, moment_part, *raw,
    )
    back = [home[0]] + [send_rep(home[NX - k], k, 0, "home") for k in range(1, NX)]
    shard = in_order(back)

    def near_half(v):
        return either(core, v[:FAR], v[FAR:])

    tokens = (mine, other)
    a = shard
    b = send(shard, to_core, "b")
    a1 = send(a, to_ring, "a1")
    part_b = send(shard, to_cross, "part_b")
    (b,) = fence((b,))
    b1 = send(b, to_ring, "b1")
    (a1,) = fence((a1,), b)
    a2 = send(a1, to_ring, "a2")
    side1 = send(a1, to_side, "side1")
    (part_b,) = fence((part_b,), a1)
    part_b1 = send(part_b, to_ring, "part_b1")
    (b1,) = fence((b1,), part_b)
    b2 = send(b1, to_ring, "b2")
    (a2,) = fence((a2,), b1)
    a3 = send(a2, to_ring, "a3")
    side2 = send(a2, to_side, "side2")
    (part_b1,) = fence((part_b1,), a2)
    part_b2 = send(part_b1, to_ring, "part_b2")
    *totals, mark = product_step(
        ((0, 1), (0, 0), (1, 0)), tokens, (a1, b1, a, part_b),
        ((0, 0, ROWS, 0, A_ROWS), (1, 0, ROWS, 0, B_ROWS), (2, 0, ROWS, 1, A_ROWS), (3, 0, ROWS, 2, B_ROWS)),
        ((1, B_ROWS, ROWS), (2, A_ROWS, ROWS)), (),
    )
    (b2,) = fence((b2,), part_b1, mark)
    b3 = send(b2, to_ring, "b3")
    (a3,) = fence((a3,), b2)
    a4 = send(near_half(a3), to_ring, "a4")
    side3 = send(a3, to_side, "side3")
    (gradient,) = fence((gradient,), a3)
    sums = [send_rep(gradient, k, 0, "gradient") for k in range(1, NX)]
    (part_b2,) = fence((part_b2,), a3)
    part_b3 = send(part_b2, to_ring, "part_b3")
    *totals, mark = product_step(
        ((0, 2), (1, 2), (1, 1)), tokens,
        (a2, b2, side2, part_b2, side1, part_b1),
        (
            (0, 0, ROWS, 0, A_ROWS), (1, 0, ROWS, 0, B_ROWS),
            (2, 0, ROWS, 1, A_ROWS), (3, 0, ROWS, 1, B_ROWS),
            (4, 0, ROWS, 2, A_ROWS), (5, 0, ROWS, 2, B_ROWS),
        ),
        (), totals,
    )
    (b3,) = fence((b3,), part_b2, mark)
    b4 = send(near_half(b3), to_ring, "b4")
    far_side = send(a4, to_side, "far_side")
    (part_b3,) = fence((part_b3,), b3, b4)
    part_b4 = send(near_half(part_b3), to_ring, "part_b4")
    *totals, mark = product_step(
        ((0, 3), (1, 3)), tokens, (a3, b3, side3, part_b3),
        (
            (0, 0, ROWS, 0, A_ROWS), (1, 0, ROWS, 0, B_ROWS),
            (2, 0, ROWS, 1, A_ROWS), (3, 0, ROWS, 1, B_ROWS),
        ),
        (), totals,
    )
    total, late, _ = product_step(
        ((0, 4), (1, 4)), tokens, (a4, b4, far_side, part_b4),
        (
            (0, 0, FAR, 0, A_NEAR), (1, 0, FAR, 0, B_NEAR),
            (2, 0, FAR, 1, A_NEAR), (3, 0, FAR, 1, B_NEAR),
        ),
        tuple((s, place, FAR) for s in range(2) for place in (A_REST, B_REST)), totals, final=True,
    )
    late = send(late, to_core, "late")

    new_global, new_moment = update(global_w, momentum, in_order([gradient, *sums]))
    new_local = blend(local, new_global)
    projected = ((total + late.astype(jnp.float32)) * SCALE).astype(jnp.bfloat16)
    return (new_global, new_moment, new_local[None], projected[None])


def solution(mesh):
    return jax.shard_map(
        on_device,
        mesh=mesh,
        in_specs=(P("fsdp", None), P("fsdp", None), P("rep", "fsdp", None), P("rep", "fsdp", None)),
        out_specs=(
            P("fsdp", None),
            P("fsdp", None),
            P("rep", "fsdp", None),
            P("rep", "fsdp", None),
        ),
        check_vma=False,
    )
```
